256 devices in a mesh: ctx: 64 (over x, z, core), fsdp: 4 (over y).
Axes of the slice: x: 4, y: 4, z: 8, core: 2. Of those that a mesh axis runs over, the one named last changes fastest.
Arguments:
- tokens: bfloat16 [4, 8192, 4096], P('fsdp', 'ctx'), may hold values from -48 to 48
- w_query: bfloat16 [4096, 2048], P(('ctx', 'fsdp')), may hold values from -0.09375 to 0.09375
- w_key: bfloat16 [4096, 512], P(('ctx', 'fsdp')), may hold values from -0.09375 to 0.09375
- w_value: bfloat16 [4096, 512], P(('ctx', 'fsdp')), may hold values from -0.09375 to 0.09375
- doc_starts: int32 [4, 71], P('fsdp'), may hold values from 0 to 8192, as said below
- crossing: int32 [4, 64, 7], P('fsdp', 'ctx'), may hold values from 0 to 1, as said below
Outputs:
- attended: bfloat16 [4, 8192, 2048], P('fsdp', 'ctx')
The draws below stay inside these ranges and needn't reach their ends.
Inputs may be any that keep to these rules, and one draw needn't show every extreme that they name: `doc_starts`: each row begins with 0 and rises strictly through the starts of the sequence's documents, then holds 8192 in the remaining slots; every document holds 1 to 896 tokens, and one document of every sequence holds exactly 896. crossing[q, s, k - 1] is 1 exactly when shard s - k of sequence q exists and holds a token of the document that contains the first token of shard s.
All inputs are finite; a program needn't handle non-finite values.
Results may differ from the reference program's by a relative error of at most 0.023.
Values may be sent and summed in bfloat16 or wider, within the bound.
A program may use at most 128 MiB of HBM per device.

```python
import jax
import jax.numpy as jnp
from jax import lax

D = 4096
HD = 128
GROUP = 4
KVH = 4
SPAN = 7
KMAX = 6
TOK_DEV = 128
BATCH_ROWS = 4
TOKENS_PER_ROW = 8192
NBLK = 10
MAXDOC = 896
QW = 2048
KVW = 512
N_CTX = 64


def sequence_layout(key):
    key_offset, key_counts, key_whole, key_places, key_flip = jax.random.split(key, 5)
    inner_offset = jax.random.randint(key_offset, (), 1, TOK_DEV)
    flipped = jax.random.randint(key_flip, (), 0, 2) == 1
    offset = jnp.where(flipped, TOK_DEV, inner_offset).astype(jnp.int32)
    bounds = offset + jnp.arange(NBLK, dtype=jnp.int32) * MAXDOC
    counts = jax.random.randint(key_counts, (NBLK,), 0, KMAX + 1)
    whole_block = jax.random.randint(key_whole, (), 0, (N_CTX - 1) // SPAN)
    counts = jnp.where(jnp.arange(NBLK) == whole_block, 0, counts)

    def block_places(block_key):
        return jax.random.permutation(block_key, MAXDOC - 1)[:KMAX] + 1
    chosen = jax.vmap(block_places)(jax.random.split(key_places, NBLK))
    candidate = bounds[:, None] + chosen
    usable = (jnp.arange(KMAX)[None, :] < counts[:, None]) & (candidate < TOKENS_PER_ROW)
    candidate = jnp.where(usable, candidate, TOKENS_PER_ROW)
    edges = jnp.where(bounds < TOKENS_PER_ROW, bounds, TOKENS_PER_ROW)
    merged = jnp.concatenate([jnp.zeros((1,), jnp.int32), edges.astype(jnp.int32), candidate.reshape(-1).astype(jnp.int32)])
    return jnp.sort(merged).astype(jnp.int32)


def document_layout(key):
    return jax.vmap(sequence_layout)(jax.random.split(key, BATCH_ROWS))


def draw_doc_starts(key, part):
    return document_layout(key)


def draw_crossing(key, part):
    begins = document_layout(key)
    shard_first = jnp.arange(N_CTX, dtype=jnp.int32) * TOK_DEV

    def one_row(row_starts):
        doc_first = jnp.max(jnp.where(row_starts[None, :] <= shard_first[:, None], row_starts[None, :], 0), axis=1)
        distance = jnp.arange(1, SPAN + 1, dtype=jnp.int32)
        source = jnp.arange(N_CTX, dtype=jnp.int32)[:, None] - distance[None, :]
        reached = (source >= 0) & (doc_first[:, None] < (source + 1) * TOK_DEV)
        return reached.astype(jnp.int32)
    return jax.vmap(one_row)(begins)


def draw_tokens(key, part):
    key = jax.random.fold_in(key, 11)
    lookup_resting_offset = jax.random.fold_in(key, 0)
    shape = (BATCH_ROWS, TOKENS_PER_ROW, D)
    payload_elements = jnp.clip(jax.random.normal(lookup_resting_offset, shape, jnp.float32), -6.0, 6.0)
    return payload_elements.astype(jnp.bfloat16)


def shard_levels(rng, shape, pieces, smallest, largest):
    def one(position, parts):
        draws = jax.random.uniform(jax.random.fold_in(jax.random.fold_in(rng, 6), position), (parts,), jnp.float32, smallest / len(pieces), largest / len(pieces))
        return jnp.repeat(jnp.exp(draws), shape[position] // parts).reshape((-1,) + (1,) * (len(shape) - position - 1))

    factor_of = one(*pieces[0])
    for cut in pieces[1:]:
        factor_of = factor_of * one(*cut)
    return factor_of


def gaussian(key, extent, deviation, bound, cuts=(), kind=jnp.bfloat16):
    result = deviation * jax.random.normal(key, extent, jnp.float32)
    if cuts:
        result = result * shard_levels(key, extent, cuts, -0.22, 0.18)
    return jnp.clip(result, -bound, bound).astype(kind)


def setup_inputs(seed: int = 0) -> dict:
    keys = jax.random.split(jax.random.key(seed), 7)
    tokens = draw_tokens(jax.random.fold_in(keys[6], 71), 0)
    w_query = gaussian(keys[1], (D, QW), D ** -0.5, 0.09375, ((0, 256),))
    w_key = gaussian(keys[2], (D, KVW), D ** -0.5, 0.09375, ((0, 256),))
    w_value = gaussian(keys[3], (D, KVW), D ** -0.5, 0.09375, ((0, 256),))
    doc_starts = draw_doc_starts(jax.random.fold_in(keys[6], 71), 0)
    crossing = draw_crossing(jax.random.fold_in(keys[6], 71), 0)
    return dict(tokens=tokens, w_query=w_query, w_key=w_key, w_value=w_value, doc_starts=doc_starts, crossing=crossing)


theta_base = 500000.0


def rotate(vectors, positions):
    half_dim = vectors.shape[-1] // 2
    frequency = theta_base ** (-(jnp.arange(half_dim, dtype=jnp.float32) * 2.0) / vectors.shape[-1])
    angles = positions.astype(jnp.float32)[:, None] * frequency[None, :]
    cos_table = jnp.cos(angles)[:, None, :]
    sin_table = jnp.sin(angles)[:, None, :]
    lower_half = vectors[..., :half_dim]
    upper_half = vectors[..., half_dim:]
    return jnp.concatenate([lower_half * cos_table - upper_half * sin_table, upper_half * cos_table + lower_half * sin_table], axis=-1)


def doc_index(positions, doc_begin):
    return jnp.sum((doc_begin[None, :] <= positions[:, None]).astype(jnp.int32), axis=1) - 1


def allowed(query_at, key_at, doc_begin, crossed, shard_index, row_count, reach_count):
    query_doc = doc_index(query_at, doc_begin)
    key_doc = doc_index(key_at, doc_begin)
    distance = shard_index - jnp.floor_divide(key_at, row_count)
    picked = crossed[jnp.clip(distance - 1, 0, reach_count - 1)]
    opened = jnp.where(distance == 0, 1, jnp.where(distance > reach_count, 0, picked))
    causal = key_at[None, :] <= query_at[:, None]
    return causal & (key_at >= 0)[None, :] & (query_doc[:, None] == key_doc[None, :]) & (opened == 1)[None, :]


def softmax_rows(scores, allowed_map):
    masked = jnp.where(allowed_map, scores, -1e30)
    highest = jnp.max(masked, axis=-1, keepdims=True)
    raised = jnp.where(allowed_map, jnp.exp(masked - highest), 0.0)
    return (raised / jnp.sum(raised, axis=-1, keepdims=True)).astype(jnp.bfloat16)


def reference(tokens, w_query, w_key, w_value, doc_starts, crossing):
    scaling = HD ** -0.5
    head_count = KVH * GROUP
    padding = SPAN * TOK_DEV
    results = []
    for sequence in range(BATCH_ROWS):
        inputs = tokens[sequence]
        queries = jnp.dot(inputs, w_query, preferred_element_type=jnp.float32)
        key_proj = jnp.dot(inputs, w_key, preferred_element_type=jnp.float32)
        value_proj = jnp.dot(inputs, w_value, preferred_element_type=jnp.float32)
        positions = jnp.arange(TOKENS_PER_ROW, dtype=jnp.int32)
        query_rot = rotate(queries.reshape(TOKENS_PER_ROW, head_count, HD), positions).astype(jnp.bfloat16)
        key_rot = rotate(key_proj.reshape(TOKENS_PER_ROW, KVH, HD), positions).astype(jnp.bfloat16)
        value_rows = value_proj.reshape(TOKENS_PER_ROW, KVH, HD).astype(jnp.bfloat16)
        key_padded = jnp.concatenate([jnp.zeros((padding, KVH, HD), jnp.bfloat16), key_rot], axis=0)
        value_padded = jnp.concatenate([jnp.zeros((padding, KVH, HD), jnp.bfloat16), value_rows], axis=0)
        doc_begin = doc_starts[sequence]
        crossed_all = crossing[sequence]

        def one_shard(shard_index):
            first_row = (shard_index * TOK_DEV).astype(jnp.int32)
            query_block = lax.dynamic_slice_in_dim(query_rot, first_row, TOK_DEV, 0)
            key_window = lax.dynamic_slice_in_dim(key_padded, first_row, padding + TOK_DEV, 0)
            value_window = lax.dynamic_slice_in_dim(value_padded, first_row, padding + TOK_DEV, 0)
            query_at = first_row + jnp.arange(TOK_DEV, dtype=jnp.int32)
            key_at = first_row - padding + jnp.arange(padding + TOK_DEV, dtype=jnp.int32)
            crossed = crossed_all[shard_index]
            allowed_map = allowed(query_at, key_at, doc_begin, crossed, shard_index, TOK_DEV, SPAN)
            key_repeat = jnp.repeat(key_window, GROUP, axis=1).astype(jnp.float32)
            value_repeat = jnp.repeat(value_window, GROUP, axis=1).astype(jnp.float32)
            scores = jnp.einsum("qhd,khd->hqk", query_block.astype(jnp.float32), key_repeat) * scaling
            attention = softmax_rows(scores, allowed_map[None, :, :])
            context = jnp.einsum("hqk,khd->qhd", attention.astype(jnp.float32), value_repeat)
            return context.astype(jnp.bfloat16).reshape(TOK_DEV, head_count * HD)

        context_all = lax.map(one_shard, jnp.arange(N_CTX, dtype=jnp.int32)).reshape(TOKENS_PER_ROW, head_count * HD)
        results.append(context_all)
    return jnp.stack(results, axis=0)
```

```python
import functools

import jax
import jax.numpy as jnp
import numpy as np
from jax import lax
from jax.experimental import pallas as pl
from jax.experimental.pallas import tpu as pltpu
from jax.sharding import PartitionSpec as P

MESH = pl.DeviceIdType.MESH
NX, NY, NZ = 4, 4, 8
ROWS = 128
D = 4096
HD = 128
GROUP = 4
REACH = 7
QC = GROUP * HD
COLS = 2 * HD + QC
WINDOW = (REACH + 1) * ROWS
OFFSETS = (0, 1, 3, 2)
SLOT_OF = {0: 0, 1: 1, 3: 2, 2: 3}
THETA = 500000.0
SCALE = HD ** -0.5
NEG = -1e30


def tables():
    freq = THETA ** (-(np.arange(HD // 2) * 2.0) / HD)
    freq = np.concatenate([freq, freq])
    rows = np.arange(ROWS)[:, None] * freq[None, :]
    shards = (np.arange(NX * NZ * 2) * ROWS)[:, None] * freq[None, :]
    row_tab = np.stack([np.cos(rows), np.sin(rows)]).astype(np.float32)
    shard_tab = np.stack([np.cos(shards), np.sin(shards)], axis=1).astype(np.float32)
    return row_tab, shard_tab


def kernel(
    tok_in, wq_in, wk_in, wv_in, starts, opened, row_tab, shard_tab,
    out,
    tok, w, kv, q, att, opens,
    loc_sem, tok_s, tok_r, a_s, a_r, z_s, z_r, y_s, y_r, c_s, c_r, h_s, h_r, hc_s, hc_r, o_s, o_r,
):
    ctx = lax.axis_index("ctx")
    y = lax.axis_index("fsdp")
    x = ctx // (2 * NZ)
    z = lax.rem(ctx // 2, NZ)
    c = lax.rem(ctx, 2)
    o = 1 - c

    def dev(px, py, pz, pc):
        return ((px * NZ + pz) * 2 + pc, py)

    def xs(k):
        return lax.rem(x + k + NX, NX)

    def ys(k):
        return lax.rem(y + k + NY, NY)

    def zs(k):
        return lax.rem(z + k + NZ, NZ)

    sibling = dev(x, y, z, o)
    peers = [dev(xs(k), y, z, c) for k in (1, 2, 3)]
    peers += [dev(x, ys(k), z, c) for k in (1, 2, 3)]
    peers += [dev(x, y, zs(k), c) for k in range(1, NZ)]
    peers += [sibling, dev(x, y, zs(1), o), dev(x, y, zs(-1), o)]

    sent = []

    def send(src, dst, ssem, rsem, to):
        cp = pltpu.make_async_remote_copy(
            src_ref=src, dst_ref=dst, send_sem=ssem, recv_sem=rsem, device_id=to, device_id_type=MESH
        )
        cp.start()
        sent.append(cp)
        return cp

    def arrive(dst, ssem, rsem):
        pltpu.make_async_remote_copy(
            src_ref=dst, dst_ref=dst, send_sem=ssem, recv_sem=rsem, device_id=sibling, device_id_type=MESH
        ).wait_recv()

    local = []

    def move(src, dst, sem):
        cp = pltpu.make_async_copy(src, dst, sem)
        cp.start()
        local.append(cp)
        return cp

    own_tok = move(tok_in, tok.at[0], loc_sem.at[0])
    own_open = move(opened, opens.at[0], loc_sem.at[1])
    row16 = c * 64 + y * 16
    parts = ((wk_in, HD, 0), (wv_in, HD, HD), (wq_in, QC, 2 * HD))
    own_w = [
        move(
            ref.at[:, pl.ds(pl.multiple_of(x * n, n), n)],
            w.at[x, z, pl.ds(row16, 16), pl.ds(at, n)],
            loc_sem.at[2 + i],
        )
        for i, (ref, n, at) in enumerate(parts)
    ]

    barrier = pltpu.get_barrier_semaphore()
    for peer in peers:
        pl.semaphore_signal(barrier, inc=1, device_id=peer, device_id_type=MESH)
    pl.semaphore_wait(barrier, len(peers))

    for i, (ref, n, at) in enumerate(parts):
        for k in (1, 3, 2):
            to = xs(k)
            send(
                ref.at[:, pl.ds(pl.multiple_of(to * n, n), n)],
                w.at[x, z, pl.ds(row16, 16), pl.ds(at, n)],
                a_s.at[i, k - 1], a_r.at[i, k - 1], dev(to, y, z, c),
            )
    CH = D // 4
    for j in range(4):
        for side, (k, slot, order) in enumerate(((1, 2, (0, 1, 2, 3)), (-1, 1, (2, 3, 0, 1)))):
            cols = pl.ds(order[j] * CH, CH)
            send(
                tok_in.at[:, cols], tok.at[slot, :, cols],
                tok_s.at[side, order[j]], tok_r.at[slot - 1, order[j]], dev(xs(k), y, z, c),
            )
    for k in (1, 3, 2):
        slot = SLOT_OF[(-k) % NX]
        send(opened, opens.at[slot], a_s.at[3, k - 1], a_r.at[3, slot - 1], dev(xs(k), y, z, c))

    groups = ((0, 2 * HD), (2 * HD, QC))

    def block(g, px, pz):
        at, n = groups[g]
        return w.at[px, pz, pl.ds(row16, 16), pl.ds(at, n)]

    def zline(g, py, pc, half=None):
        at, n = groups[g]
        rows = pl.ds(pc * 64 + py * 16, 16)
        if half is None:
            return w.at[:, :, rows, pl.ds(at, n)]
        return w.at[pl.ds(2 * half, 2), :, rows, pl.ds(at, n)]

    def zblock(g, pz):
        at, n = groups[g]
        return w.at[:, pz, pl.ds(row16, 16), pl.ds(at, n)]

    def stage_z(g):
        for i in (0, 1) if g == 0 else (2,):
            ref, n, at = parts[i]
            own_w[i].wait()
            for k in (1, 3, 2):
                src = xs(-k)
                arrive(w.at[src, z, pl.ds(row16, 16), pl.ds(at, n)], a_s.at[i, k - 1], a_r.at[i, k - 1])
        for k in (1, 7, 2, 6, 3, 5, 4):
            send(zblock(g, z), zblock(g, z), z_s.at[g, k - 1], z_r.at[g, k - 1], dev(x, y, zs(k), c))

    def stage_y(g):
        for k in (1, 7, 2, 6, 3, 5, 4):
            arrive(zblock(g, zs(-k)), z_s.at[g, k - 1], z_r.at[g, k - 1])
        for j in range(2):
            for side, k in enumerate((1, -1)):
                half = j if side == 0 else 1 - j
                line = zline(g, y, c, half)
                send(line, line, y_s.at[g, side, half], y_r.at[g, side, half], dev(x, ys(k), z, c))
        line = zline(g, y, c)
        send(line, line, c_s.at[g, 0], c_r.at[g, 0], sibling)

    def stage_forward(g):
        for side, k in enumerate((-1, 1)):
            line = zline(g, ys(k), c, side)
            arrive(line, y_s.at[g, side, side], y_r.at[g, side, side])
            send(line, line, y_s.at[g, 2, side], y_r.at[g, 2, side], dev(x, ys(-k), z, c))

    def stage_share(g):
        for side, k in enumerate((-1, 1)):
            arrive(zline(g, ys(k), c, 1 - side), y_s.at[g, side, 1 - side], y_r.at[g, side, 1 - side])
            line = zline(g, ys(k), c)
            send(line, line, c_s.at[g, 1 + side], c_r.at[g, 1 + side], sibling)
        for half in range(2):
            arrive(zline(g, ys(2), c, half), y_s.at[g, 2, half], y_r.at[g, 2, half])
        line = zline(g, ys(2), c)
        send(line, line, c_s.at[g, 3], c_r.at[g, 3], sibling)

    def stage_end(g):
        for i, k in enumerate((0, -1, 1, 2)):
            arrive(zline(g, ys(k), o), c_s.at[g, i], c_r.at[g, i])

    def forward_tokens(j):
        for side, (slot, k) in enumerate(((2, 1), (1, -1))):
            n = 2 * side + j
            cols = pl.ds(n * CH, CH)
            arrive(tok.at[slot, :, cols], tok_s.at[side, n], tok_r.at[slot - 1, n])
            send(tok.at[slot, :, cols], tok.at[3, :, cols], tok_s.at[2, n], tok_r.at[2, n], dev(xs(k), y, z, c))

    stage_z(0)
    stage_z(1)
    stage_y(0)
    forward_tokens(0)
    stage_forward(0)
    forward_tokens(1)
    stage_y(1)
    stage_share(0)
    stage_forward(1)
    stage_end(0)
    for side, slot in enumerate((2, 1)):
        for n in (2 - 2 * side, 3 - 2 * side):
            cols = pl.ds(n * CH, CH)
            arrive(tok.at[slot, :, cols], tok_s.at[side, n], tok_r.at[slot - 1, n])
    own_tok.wait()

    cos_row, sin_row = row_tab[0], row_tab[1]
    sign = jnp.where(lax.broadcasted_iota(jnp.int32, (1, HD), 1) < HD // 2, -1.0, 1.0).astype(jnp.float32)

    def shard_of(p):
        return xs(OFFSETS[p]) * (2 * NZ) + z * 2 + c

    def rotary(p):
        tab = shard_tab[shard_of(p)]
        ca, sa = tab[0:1, :], tab[1:2, :]
        return ca * cos_row - sa * sin_row, (sa * cos_row + ca * sin_row) * sign

    def rotate(v, cs, sn):
        return v * cs + pltpu.roll(v, HD // 2, 1) * sn

    def project(first, count, at, n):
        total = None
        for j in range(4):
            rows = tok[first:first + count, :, j * CH:(j + 1) * CH].reshape(count * ROWS, CH)
            cols = w[j, :, :, at:at + n].reshape(CH, n)
            part = jnp.dot(rows, cols, preferred_element_type=jnp.float32)
            total = part if total is None else total + part
        return total

    wrap = jnp.where(z == NZ - 1, 1, 0)

    def slot_ahead(p):
        turned = SLOT_OF[(OFFSETS[p] + 1) % NX]
        return jnp.where(wrap == 1, turned, p)

    def send_own(p):
        tile = kv.at[p, 8 + c]
        send(tile, tile, hc_s.at[p, 0], hc_r.at[p, 0], sibling)
        n = slot_ahead(p)
        send(tile, kv.at[n, 6 + c], h_s.at[p, 0], h_r.at[n, 0], dev(x, y, zs(1), c))

    def keys(first, count):
        total = project(first, count, 0, 2 * HD)
        for i in range(count):
            p = first + i
            part = total[i * ROWS:(i + 1) * ROWS]
            cs, sn = rotary(p)
            kv[p, 8 + c, :, 0:HD] = rotate(part[:, 0:HD], cs, sn).astype(jnp.bfloat16)
            kv[p, 8 + c, :, HD:2 * HD] = part[:, HD:2 * HD].astype(jnp.bfloat16)
            send_own(p)

    def queries(first, count):
        total = project(first, count, 2 * HD, QC)
        for i in range(count):
            p = first + i
            part = total[i * ROWS:(i + 1) * ROWS]
            cs, sn = rotary(p)
            for h in range(GROUP):
                head = part[:, h * HD:(h + 1) * HD]
                q[p, h] = rotate(head, cs, sn).astype(jnp.bfloat16)

    last = []

    def pass_on(p, d):
        tile = kv.at[p, 2 * (4 - d) + c]
        arrive(tile, h_s.at[p, d - 1], h_r.at[p, d - 1])
        n = slot_ahead(p)
        if d < 3:
            send(tile, kv.at[n, 2 * (3 - d) + c], h_s.at[p, d], h_r.at[n, d], dev(x, y, zs(1), c))
        else:
            cp = pltpu.make_async_remote_copy(
                src_ref=kv.at[p, 3], dst_ref=kv.at[n, 1], send_sem=h_s.at[p, 3], recv_sem=h_r.at[n, 3],
                device_id=dev(x, y, zs(1), 0), device_id_type=MESH,
            )
            last.append(cp)

            @pl.when(c == 1)
            def _():
                cp.start()
        send(tile, tile, hc_s.at[p, d], hc_r.at[p, d], sibling)

    def gather_keys(p):
        for d in range(4):
            arrive(kv.at[p, 2 * (4 - d) + o], hc_s.at[p, d], hc_r.at[p, d])

        @pl.when(c == 0)
        def _():
            arrive(kv.at[p, 1], h_s.at[p, 3], h_r.at[p, 3])

    def attend(p):
        s = shard_of(p)
        q_at = (s * ROWS + lax.broadcasted_iota(jnp.int32, (ROWS, 1), 0)).astype(jnp.float32)
        begin = jnp.max(jnp.where(starts[...] <= q_at, starts[...], 0.0), axis=1, keepdims=True)
        k_at = ((s - REACH) * ROWS + lax.broadcasted_iota(jnp.int32, (1, WINDOW), 1)).astype(jnp.float32)
        k_at = jnp.where(opens[p] == 1, k_at, -1.0)
        seen = (k_at <= q_at) & (k_at >= begin)
        k_all = kv[p, pl.ds(1 + c, 8), :, 0:HD].reshape(WINDOW, HD)
        v_all = kv[p, pl.ds(1 + c, 8), :, HD:2 * HD].reshape(WINDOW, HD)
        for h in range(GROUP):
            scores = lax.dot_general(
                q[p, h], k_all, (((1,), (1,)), ((), ())), preferred_element_type=jnp.float32
            ) * SCALE
            scores = jnp.where(seen, scores, NEG)
            top = jnp.max(scores, axis=1, keepdims=True)
            raised = jnp.exp(scores - top)
            total = jnp.sum(raised, axis=1, keepdims=True)
            mixed = jnp.dot(raised.astype(jnp.bfloat16), v_all, preferred_element_type=jnp.float32)
            att[p, :, h * HD:(h + 1) * HD] = (mixed / total).astype(jnp.bfloat16)
        mine = out.at[:, pl.ds(pl.multiple_of(x * QC, QC), QC)]
        k = OFFSETS[p]
        if k == 0:
            move(att.at[p], mine, loc_sem.at[5])
        else:
            send(att.at[p], mine, o_s.at[k - 1], o_r.at[k - 1], dev(xs(k), y, z, c))

    keys(0, 3)
    stage_share(1)
    for j in range(4):
        cols = pl.ds(j * CH, CH)
        arrive(tok.at[3, :, cols], tok_s.at[2, j], tok_r.at[2, j])
    keys(3, 1)
    stage_end(1)
    for p in (0, 1):
        for d in (1, 2, 3):
            pass_on(p, d)
    queries(0, 3)
    for p in (2, 3):
        for d in (1, 2, 3):
            pass_on(p, d)
    queries(3, 1)
    own_open.wait()
    for slot in (1, 2, 3):
        arrive(opens.at[slot], a_s.at[3, slot - 1], a_r.at[3, slot - 1])
    for p in (1, 0, 2, 3):
        gather_keys(p)
        attend(p)

    for k in (1, 3, 2):
        src = xs(-k)
        arrive(out.at[:, pl.ds(pl.multiple_of(src * QC, QC), QC)], o_s.at[k - 1], o_r.at[k - 1])
    local[-1].wait()
    for cp in sent:
        cp.wait_send()
    for cp in last:
        @pl.when(c == 1)
        def _(cp=cp):
            cp.wait_send()


def local(tokens, w_query, w_key, w_value, doc_starts, crossing):
    row_tab, shard_tab = tables()
    starts = jnp.pad(doc_starts, ((0, 0), (0, HD - doc_starts.shape[1])), constant_values=NX * NZ * 2 * ROWS)
    starts = starts.astype(jnp.float32)
    opened = jnp.concatenate([crossing[0, :, ::-1], jnp.ones((1, 1), jnp.int32)], axis=1)
    opened = jnp.repeat(opened, ROWS, axis=1)
    anyw = pl.BlockSpec(memory_space=pl.ANY)
    vmem = pl.BlockSpec(memory_space=pltpu.VMEM)
    dma = pltpu.SemaphoreType.DMA
    bf16 = jnp.bfloat16
    out = pl.pallas_call(
        kernel,
        out_shape=jax.ShapeDtypeStruct((ROWS, NX * QC), bf16),
        in_specs=[anyw, anyw, anyw, anyw, vmem, vmem, vmem, vmem],
        out_specs=anyw,
        scratch_shapes=[
            pltpu.VMEM((4, ROWS, D), bf16),
            pltpu.VMEM((NX, NZ, ROWS, COLS), bf16),
            pltpu.VMEM((4, 10, ROWS, 2 * HD), bf16),
            pltpu.VMEM((4, GROUP, ROWS, HD), bf16),
            pltpu.VMEM((4, ROWS, QC), bf16),
            pltpu.VMEM((4, 1, WINDOW), jnp.int32),
            dma((6,)),
            dma((3, 4)), dma((3, 4)),
            dma((4, 3)), dma((4, 3)),
            dma((2, 7)), dma((2, 7)),
            dma((2, 3, 2)), dma((2, 3, 2)),
            dma((2, 4)), dma((2, 4)),
            dma((4, 4)), dma((4, 4)),
            dma((4, 4)), dma((4, 4)),
            dma((3,)), dma((3,)),
        ],
        compiler_params=pltpu.CompilerParams(
            collective_id=0, has_side_effects=True, vmem_limit_bytes=48 << 20
        ),
    )(
        tokens.reshape(ROWS, D), w_query, w_key, w_value, starts, opened,
        jnp.asarray(row_tab), jnp.asarray(shard_tab),
    )
    return out.reshape(1, ROWS, NX * QC)


def solution(mesh):
    return jax.shard_map(
        local,
        mesh=mesh,
        in_specs=(
            P("fsdp", "ctx", None),
            P(("ctx", "fsdp"), None),
            P(("ctx", "fsdp"), None),
            P(("ctx", "fsdp"), None),
            P("fsdp", None),
            P("fsdp", "ctx", None),
        ),
        out_specs=P("fsdp", "ctx", None),
        check_vma=False,
    )
```

```python
import functools

import jax
import jax.numpy as jnp
import numpy as np
from jax import lax
from jax.experimental import pallas as pl
from jax.experimental.pallas import tpu as pltpu
from jax.sharding import PartitionSpec as P

MESH = pl.DeviceIdType.MESH
NX, NY, NZ = 4, 4, 8
ROWS = 128
D = 4096
HD = 128
GROUP = 4
REACH = 7
QC = GROUP * HD
COLS = 2 * HD + QC
WINDOW = (REACH + 1) * ROWS
OFFSETS = (0, 1, 3, 2)
SLOT_OF = {0: 0, 1: 1, 3: 2, 2: 3}
THETA = 500000.0
SCALE = HD ** -0.5
NEG = -1e30


def tables():
    freq = THETA ** (-(np.arange(HD // 2) * 2.0) / HD)
    freq = np.concatenate([freq, freq])
    at = np.concatenate([np.arange(ROWS), np.arange(NX * NZ * 2) * ROWS])
    angles = at[:, None] * freq[None, :]
    return np.stack([np.cos(angles), np.sin(angles)]).astype(np.float32)


def kernel(
    tok_in, wq_in, wk_in, wv_in, starts_in, crossing, tab_in,
    out,
    tok, w, kv, q, att, opens, tab, starts,
    loc_sem, tok_s, tok_r, a_s, a_r, z_s, z_r, y_s, y_r, c_s, c_r, h_s, h_r, hc_s, hc_r, o_s, o_r,
):
    ctx = lax.axis_index("ctx")
    y = lax.axis_index("fsdp")
    x = ctx // (2 * NZ)
    z = lax.rem(ctx // 2, NZ)
    c = lax.rem(ctx, 2)
    o = 1 - c

    def dev(px, py, pz, pc):
        return ((px * NZ + pz) * 2 + pc, py)

    def xs(k):
        return lax.rem(x + k + NX, NX)

    def ys(k):
        return lax.rem(y + k + NY, NY)

    def zs(k):
        return lax.rem(z + k + NZ, NZ)

    sibling = dev(x, y, z, o)
    peers = [dev(xs(k), y, z, c) for k in (1, 2, 3)]
    peers += [dev(x, ys(k), z, c) for k in (1, 2, 3)]
    peers += [dev(x, y, zs(k), c) for k in range(1, NZ)]
    peers += [sibling, dev(x, y, zs(1), o), dev(x, y, zs(-1), o)]

    sent = []

    def send(src, dst, ssem, rsem, to):
        cp = pltpu.make_async_remote_copy(
            src_ref=src, dst_ref=dst, send_sem=ssem, recv_sem=rsem, device_id=to, device_id_type=MESH
        )
        cp.start()
        sent.append(cp)
        return cp

    def arrive(dst, ssem, rsem):
        pltpu.make_async_remote_copy(
            src_ref=dst, dst_ref=dst, send_sem=ssem, recv_sem=rsem, device_id=sibling, device_id_type=MESH
        ).wait_recv()

    local = []

    def move(src, dst, sem):
        cp = pltpu.make_async_copy(src, dst, sem)
        cp.start()
        local.append(cp)
        return cp

    own_tok = move(tok_in, tok.at[0], loc_sem.at[0])
    own_tab = move(tab_in, tab, loc_sem.at[1])
    own_starts = move(starts_in, starts, loc_sem.at[6])
    row16 = c * 64 + y * 16
    parts = ((wk_in, HD, 0), (wv_in, HD, HD), (wq_in, QC, 2 * HD))
    own_w = [
        move(
            ref.at[:, pl.ds(pl.multiple_of(x * n, n), n)],
            w.at[x, z, pl.ds(row16, 16), pl.ds(at, n)],
            loc_sem.at[2 + i],
        )
        for i, (ref, n, at) in enumerate(parts)
    ]

    barrier = pltpu.get_barrier_semaphore()
    for peer in peers:
        pl.semaphore_signal(barrier, inc=1, device_id=peer, device_id_type=MESH)
    for k in range(REACH):
        opens[0, :, k * ROWS:(k + 1) * ROWS] = jnp.full((1, ROWS), crossing[0, 0, REACH - 1 - k], jnp.int32)
    opens[0, :, REACH * ROWS:] = jnp.ones((1, ROWS), jnp.int32)
    pl.semaphore_wait(barrier, len(peers))

    for i, (ref, n, at) in enumerate(parts):
        for k in (1, 3, 2):
            to = xs(k)
            send(
                ref.at[:, pl.ds(pl.multiple_of(to * n, n), n)],
                w.at[x, z, pl.ds(row16, 16), pl.ds(at, n)],
                a_s.at[i, k - 1], a_r.at[i, k - 1], dev(to, y, z, c),
            )
    CH = D // 4
    for j in range(4):
        for side, (k, slot, order) in enumerate(((1, 2, (0, 1, 2, 3)), (-1, 1, (2, 3, 0, 1)))):
            cols = pl.ds(order[j] * CH, CH)
            send(
                tok_in.at[:, cols], tok.at[slot, :, cols],
                tok_s.at[side, order[j]], tok_r.at[slot - 1, order[j]], dev(xs(k), y, z, c),
            )
    for k in (1, 3, 2):
        slot = SLOT_OF[(-k) % NX]
        send(opens.at[0], opens.at[slot], a_s.at[3, k - 1], a_r.at[3, slot - 1], dev(xs(k), y, z, c))

    groups = ((0, 2 * HD), (2 * HD, QC))

    def block(g, px, pz):
        at, n = groups[g]
        return w.at[px, pz, pl.ds(row16, 16), pl.ds(at, n)]

    def zline(g, py, pc, half=None):
        at, n = groups[g]
        rows = pl.ds(pc * 64 + py * 16, 16)
        if half is None:
            return w.at[:, :, rows, pl.ds(at, n)]
        return w.at[pl.ds(2 * half, 2), :, rows, pl.ds(at, n)]

    def zblock(g, pz):
        at, n = groups[g]
        return w.at[:, pz, pl.ds(row16, 16), pl.ds(at, n)]

    def stage_z(g):
        for i in (0, 1) if g == 0 else (2,):
            ref, n, at = parts[i]
            own_w[i].wait()
            for k in (1, 3, 2):
                src = xs(-k)
                arrive(w.at[src, z, pl.ds(row16, 16), pl.ds(at, n)], a_s.at[i, k - 1], a_r.at[i, k - 1])
        for k in (1, 7, 2, 6, 3, 5, 4):
            send(zblock(g, z), zblock(g, z), z_s.at[g, k - 1], z_r.at[g, k - 1], dev(x, y, zs(k), c))

    def stage_y(g):
        for k in (1, 7, 2, 6, 3, 5, 4):
            arrive(zblock(g, zs(-k)), z_s.at[g, k - 1], z_r.at[g, k - 1])
        for j in range(2):
            for side, k in enumerate((1, -1)):
                half = j if side == 0 else 1 - j
                line = zline(g, y, c, half)
                send(line, line, y_s.at[g, side, half], y_r.at[g, side, half], dev(x, ys(k), z, c))
        line = zline(g, y, c)
        send(line, line, c_s.at[g, 0], c_r.at[g, 0], sibling)

    def stage_forward(g):
        for side, k in enumerate((-1, 1)):
            line = zline(g, ys(k), c, side)
            arrive(line, y_s.at[g, side, side], y_r.at[g, side, side])
            send(line, line, y_s.at[g, 2, side], y_r.at[g, 2, side], dev(x, ys(-k), z, c))

    def stage_share(g):
        for side, k in enumerate((-1, 1)):
            arrive(zline(g, ys(k), c, 1 - side), y_s.at[g, side, 1 - side], y_r.at[g, side, 1 - side])
            line = zline(g, ys(k), c)
            send(line, line, c_s.at[g, 1 + side], c_r.at[g, 1 + side], sibling)
        for half in range(2):
            arrive(zline(g, ys(2), c, half), y_s.at[g, 2, half], y_r.at[g, 2, half])
        line = zline(g, ys(2), c)
        send(line, line, c_s.at[g, 3], c_r.at[g, 3], sibling)

    def stage_end(g):
        for i, k in enumerate((0, -1, 1, 2)):
            arrive(zline(g, ys(k), o), c_s.at[g, i], c_r.at[g, i])

    def forward_tokens(j):
        for side, (slot, k) in enumerate(((2, 1), (1, -1))):
            n = 2 * side + j
            cols = pl.ds(n * CH, CH)
            arrive(tok.at[slot, :, cols], tok_s.at[side, n], tok_r.at[slot - 1, n])
            send(tok.at[slot, :, cols], tok.at[3, :, cols], tok_s.at[2, n], tok_r.at[2, n], dev(xs(k), y, z, c))

    stage_z(0)
    stage_y(0)
    stage_z(1)
    forward_tokens(0)
    stage_forward(0)
    forward_tokens(1)
    stage_share(0)
    stage_y(1)
    stage_end(0)

    def side_tokens():
        for side, slot in enumerate((2, 1)):
            for n in (2 - 2 * side, 3 - 2 * side):
                cols = pl.ds(n * CH, CH)
                arrive(tok.at[slot, :, cols], tok_s.at[side, n], tok_r.at[slot - 1, n])

    own_tok.wait()
    own_tab.wait()
    own_starts.wait()
    cos_row, sin_row = tab[0, 0:ROWS], tab[1, 0:ROWS]
    sign = jnp.where(lax.broadcasted_iota(jnp.int32, (1, HD), 1) < HD // 2, -1.0, 1.0).astype(jnp.float32)

    def shard_of(p):
        return xs(OFFSETS[p]) * (2 * NZ) + z * 2 + c

    def rotary(p):
        ca = tab[0, pl.ds(ROWS + shard_of(p), 1)]
        sa = tab[1, pl.ds(ROWS + shard_of(p), 1)]
        return ca * cos_row - sa * sin_row, (sa * cos_row + ca * sin_row) * sign

    def rotate(v, cs, sn):
        return v * cs + pltpu.roll(v, HD // 2, 1) * sn

    def project(first, count, at, n, ready=None):
        total = None
        for j in (0, 2, 1, 3):
            if ready is not None:
                ready(j)
            rows = tok[first:first + count, :, j * CH:(j + 1) * CH].reshape(count * ROWS, CH)
            cols = w[j, :, :, at:at + n].reshape(CH, n)
            part = jnp.dot(rows, cols, preferred_element_type=jnp.float32)
            total = part if total is None else total + part
        return total

    wrap = jnp.where(z == NZ - 1, 1, 0)

    def slot_ahead(p):
        if isinstance(p, int):
            turned = SLOT_OF[(OFFSETS[p] + 1) % NX]
        else:
            turned = jnp.where(p == 2, SLOT_OF[(OFFSETS[2] + 1) % NX], SLOT_OF[(OFFSETS[3] + 1) % NX])
        return jnp.where(wrap == 1, turned, p)

    def send_own(p):
        tile = kv.at[p, 8 + c]
        send(tile, tile, hc_s.at[p, 0], hc_r.at[p, 0], sibling)
        n = slot_ahead(p)
        send(tile, kv.at[n, 6 + c], h_s.at[p, 0], h_r.at[n, 0], dev(x, y, zs(1), c))

    def keys(first, count, ready=None):
        total = project(first, count, 0, 2 * HD, ready)
        for i in range(count):
            p = first + i
            part = total[i * ROWS:(i + 1) * ROWS]
            cs, sn = rotary(p)
            kv[p, 8 + c, :, 0:HD] = rotate(part[:, 0:HD], cs, sn).astype(jnp.bfloat16)
            kv[p, 8 + c, :, HD:2 * HD] = part[:, HD:2 * HD].astype(jnp.bfloat16)
            send_own(p)

    def queries(first, count):
        total = project(first, count, 2 * HD, QC)
        for i in range(count):
            p = first + i
            part = total[i * ROWS:(i + 1) * ROWS]
            cs, sn = rotary(p)
            for h in range(GROUP):
                head = part[:, h * HD:(h + 1) * HD]
                q[p, h] = rotate(head, cs, sn).astype(jnp.bfloat16)

    last = []

    def pass_on(p, d):
        tile = kv.at[p, 2 * (4 - d) + c]
        arrive(tile, h_s.at[p, d - 1], h_r.at[p, d - 1])
        n = slot_ahead(p)
        if d < 3:
            send(tile, kv.at[n, 2 * (3 - d) + c], h_s.at[p, d], h_r.at[n, d], dev(x, y, zs(1), c))
        else:
            cp = pltpu.make_async_remote_copy(
                src_ref=kv.at[p, 3], dst_ref=kv.at[n, 1], send_sem=h_s.at[p, 3], recv_sem=h_r.at[n, 3],
                device_id=dev(x, y, zs(1), 0), device_id_type=MESH,
            )
            last.append(cp)

            @pl.when(c == 1)
            def _():
                cp.start()
        send(tile, tile, hc_s.at[p, d], hc_r.at[p, d], sibling)

    def gather_keys(p):
        for d in range(4):
            arrive(kv.at[p, 2 * (4 - d) + o], hc_s.at[p, d], hc_r.at[p, d])

        @pl.when(c == 0)
        def _():
            arrive(kv.at[p, 1], h_s.at[p, 3], h_r.at[p, 3])

    def attend(p):
        s = shard_of(p)
        q_at = (s * ROWS + lax.broadcasted_iota(jnp.int32, (ROWS, 1), 0)).astype(jnp.float32)
        first = starts[...].astype(jnp.float32)
        begin = jnp.max(jnp.where(first <= q_at, first, 0.0), axis=1, keepdims=True)
        k_at = ((s - REACH) * ROWS + lax.broadcasted_iota(jnp.int32, (1, WINDOW), 1)).astype(jnp.float32)
        k_at = jnp.where(opens[p] == 1, k_at, -1.0)
        seen = (k_at <= q_at) & (k_at >= begin)
        k_all = kv[p, pl.ds(1 + c, 8), :, 0:HD].reshape(WINDOW, HD)
        v_all = kv[p, pl.ds(1 + c, 8), :, HD:2 * HD].reshape(WINDOW, HD)
        for h in range(GROUP):
            scores = lax.dot_general(
                q[p, h], k_all, (((1,), (1,)), ((), ())), preferred_element_type=jnp.float32
            ) * SCALE
            scores = jnp.where(seen, scores, NEG)
            top = jnp.max(scores, axis=1, keepdims=True)
            raised = jnp.exp(scores - top)
            total = jnp.sum(raised, axis=1, keepdims=True)
            mixed = jnp.dot(raised.astype(jnp.bfloat16), v_all, preferred_element_type=jnp.float32)
            att[p, :, h * HD:(h + 1) * HD] = (mixed / total).astype(jnp.bfloat16)
        mine = out.at[:, pl.ds(pl.multiple_of(x * QC, QC), QC)]
        k = OFFSETS[p]
        if k == 0:
            move(att.at[p], mine, loc_sem.at[5])
        else:
            send(att.at[p], mine, o_s.at[k - 1], o_r.at[k - 1], dev(xs(k), y, z, c))

    def last_tokens(j):
        arrive(tok.at[3, :, pl.ds(j * CH, CH)], tok_s.at[2, j], tok_r.at[2, j])

    def early(d):
        for p in (0, 1, jnp.where(z < d, 3, 2)):
            pass_on(p, d)

    def late(d):
        pass_on(jnp.where(z < d, 2, 3), d)

    keys(0, 1)
    side_tokens()
    keys(1, 2)
    early(1)
    stage_forward(1)
    early(2)
    keys(3, 1, last_tokens)
    late(1)
    early(3)
    stage_share(1)
    late(2)
    stage_end(1)
    queries(0, 3)
    for slot in (1, 2, 3):
        arrive(opens.at[slot], a_s.at[3, slot - 1], a_r.at[3, slot - 1])
    late(3)
    gather_keys(1)
    attend(1)
    queries(3, 1)
    gather_keys(0)
    attend(0)
    for p in (2, 3):
        gather_keys(p)
        attend(p)

    for k in (1, 3, 2):
        src = xs(-k)
        arrive(out.at[:, pl.ds(pl.multiple_of(src * QC, QC), QC)], o_s.at[k - 1], o_r.at[k - 1])
    local[-1].wait()
    for cp in sent:
        cp.wait_send()
    for cp in last:
        @pl.when(c == 1)
        def _(cp=cp):
            cp.wait_send()


def local(tokens, w_query, w_key, w_value, doc_starts, crossing):
    anyw = pl.BlockSpec(memory_space=pl.ANY)
    dma = pltpu.SemaphoreType.DMA
    bf16 = jnp.bfloat16
    out = pl.pallas_call(
        kernel,
        out_shape=jax.ShapeDtypeStruct((ROWS, NX * QC), bf16),
        in_specs=[anyw, anyw, anyw, anyw, anyw, pl.BlockSpec(memory_space=pltpu.SMEM), anyw],
        out_specs=anyw,
        scratch_shapes=[
            pltpu.VMEM((4, ROWS, D), bf16),
            pltpu.VMEM((NX, NZ, ROWS, COLS), bf16),
            pltpu.VMEM((4, 10, ROWS, 2 * HD), bf16),
            pltpu.VMEM((4, GROUP, ROWS, HD), bf16),
            pltpu.VMEM((4, ROWS, QC), bf16),
            pltpu.VMEM((4, 1, WINDOW), jnp.int32),
            pltpu.VMEM((2, ROWS + NX * NZ * 2, HD), jnp.float32),
            pltpu.VMEM(doc_starts.shape, jnp.int32),
            dma((7,)),
            dma((3, 4)), dma((3, 4)),
            dma((4, 3)), dma((4, 3)),
            dma((2, 7)), dma((2, 7)),
            dma((2, 3, 2)), dma((2, 3, 2)),
            dma((2, 4)), dma((2, 4)),
            dma((4, 4)), dma((4, 4)),
            dma((4, 4)), dma((4, 4)),
            dma((3,)), dma((3,)),
        ],
        compiler_params=pltpu.CompilerParams(
            collective_id=0, has_side_effects=True, vmem_limit_bytes=62 << 20
        ),
    )(
        tokens.reshape(ROWS, D), w_query, w_key, w_value, doc_starts, crossing, jnp.asarray(tables()),
    )
    return out.reshape(1, ROWS, NX * QC)


def solution(mesh):
    return jax.shard_map(
        local,
        mesh=mesh,
        in_specs=(
            P("fsdp", "ctx", None),
            P(("ctx", "fsdp"), None),
            P(("ctx", "fsdp"), None),
            P(("ctx", "fsdp"), None),
            P("fsdp", None),
            P("fsdp", "ctx", None),
        ),
        out_specs=P("fsdp", "ctx", None),
        check_vma=False,
    )
```
